32 devices in a mesh: groups: 2 (over x), wide: 8 (over z, y), narrow: 2 (over core).
Axes of the slice: x: 2, y: 2, z: 4, core: 2. Of those that a mesh axis runs over, the one named last changes fastest.
Arguments:
- splats: float32 [16, 262144], P(None, ('groups', 'wide')), parts along dimension 1, may hold values from -16 to 1024, as said below
- send_slots: int32 [16, 2, 8192], P(('groups', 'wide'), 'narrow'), parts along dimension 0, may hold values from 0 to 16383, as said below
- tile_lists: int32 [16, 64, 256], P(('groups', 'wide'), 'narrow'), parts along dimension 0, may hold values from 0 to 8191, as said below
- tile_lengths: int32 [16, 64], P(('groups', 'wide'), 'narrow'), parts along dimension 0, may hold values from 32 to 256, as said below
- pixel_grads: float32 [10, 16, 64, 256], P(None, ('groups', 'wide'), 'narrow'), parts along dimension 1, may hold values from -6 to 6
Outputs:
- splat_grads: float32 [16, 262144], P(None, ('groups', 'wide')), parts along dimension 1
The draws below stay inside these ranges and needn't reach their ends.
There are 2 independent parts, one for each index of `groups`. The reference program is written for one: setup_inputs(seed, part) draws one part's arguments, and reference() takes and returns one part's arrays. A program takes and returns all parts, laid end to end along the dimension named above; each array names one. Nothing has to cross between parts.
Inputs may be any that keep to these rules, and one draw needn't show every extreme that they name: send_slots[s, n, t * 1024 + c] is the local index (within the column's 16384) of the splat in slot c of what column s sends to the device of column t and half n. A splat fills at most two slots over all devices (one for each tile it is listed in); some splats fill none. `tile_lists`: receive slot s * 1024 + c of a device is slot c of what column s sends it. The first tile_lengths entries of a tile are distinct slots, and no slot is among the live entries of two tiles of one device; entries past the length are arbitrary slots. `tile_lengths`: in every draw some tile holds exactly 256 live entries. `splats`: rows 0 and 1 are a splat's centre in pixels (tile (t, r) covers x from 16 t to 16 t + 16 and y from 16 r to 16 r + 16); rows 2, 3, 4 a conic (a, b, c) with a > 0 and a c > b b; row 5 an opacity logit of at most -1; rows 6 onward its channels.
All inputs are finite; a program needn't handle non-finite values.
Results may differ from the reference program's by a relative error of at most 0.0003.
Values sent between devices are 32-bit elements; how exact they have to be, the bound alone decides.
A program may use at most 64 MiB of HBM per device.

```python
import math
import jax
import jax.numpy as jnp
from jax import lax

CH = 10
PIX = 256
K = 256
TILE_DEV = 32
COLS = 8
ROWS = 64
SLOTS = 8192
GS_DEV = 16384
CAP = 1024
N_NARROW = 2


def to_send_layout(values):
    return values.reshape(COLS, N_NARROW, COLS, CAP).transpose(2, 1, 0, 3).reshape(COLS, N_NARROW * SLOTS)


def routing(key):
    send_key, length_key, pick_key, order_key = jax.random.split(key, 4)
    coin_key = jax.random.fold_in(key, 11)
    send = jax.vmap(lambda subkey: jax.random.permutation(subkey, GS_DEV))(jax.random.split(send_key, COLS))
    send = send.reshape(COLS, N_NARROW, SLOTS).astype(jnp.int32)
    floor_key, tile_key = jax.random.split(length_key)
    lowest = jax.random.randint(floor_key, (COLS, N_NARROW, 1), K // 8, K // 2 + 1)
    lengths = jax.random.randint(tile_key, (COLS, N_NARROW, TILE_DEV), lowest, K + 1)
    fullest = jax.random.randint(pick_key, (), 0, COLS * N_NARROW * TILE_DEV)
    flat_tiles = jnp.arange(COLS * N_NARROW * TILE_DEV).reshape(COLS, N_NARROW, TILE_DEV)
    lengths = jnp.where(flat_tiles == fullest, K, lengths).astype(jnp.int32)
    order = jax.vmap(lambda subkey: jax.random.permutation(subkey, SLOTS))(jax.random.split(order_key, COLS * N_NARROW))
    order = order.reshape(COLS, N_NARROW, SLOTS).astype(jnp.int32)
    ends = jnp.cumsum(lengths, axis=2)
    starts = ends - lengths
    places = (starts[:, :, :, None] + jnp.arange(K)[None, None, None, :]) % SLOTS
    lists = jnp.take_along_axis(order, places.reshape(COLS, N_NARROW, TILE_DEV * K), axis=2).reshape(COLS, ROWS, K)
    position = jnp.argsort(order, axis=2, stable=True).astype(jnp.int32)
    tile_of = jax.vmap(jax.vmap(lambda edges, where: jnp.searchsorted(edges, where, side='right')))(ends, position)
    active = position < ends[:, :, -1:]
    fallback = jnp.arange(SLOTS)[None, None, :] % TILE_DEV
    tile_local = jnp.where(active, jnp.minimum(tile_of, TILE_DEV - 1), fallback).astype(jnp.int32)
    half_index = jnp.arange(N_NARROW)[None, :, None]
    col_index = jnp.arange(COLS)[:, None, None]
    tile_row = tile_local + half_index * TILE_DEV
    source = (jnp.arange(SLOTS) // CAP)[None, None, :]
    group = jnp.where(active, source * TILE_DEV + tile_local, COLS * TILE_DEV).astype(jnp.int32)
    device_count = COLS * N_NARROW
    flat_group = group.reshape(device_count, SLOTS)
    sorted_index = jnp.argsort(flat_group, axis=1, stable=True).astype(jnp.int32)
    sorted_group = jnp.take_along_axis(flat_group, sorted_index, axis=1)
    place_of = jnp.argsort(sorted_index, axis=1, stable=True).astype(jnp.int32)
    first_place = jax.vmap(lambda edges, query: jnp.searchsorted(edges, query, side='left'))(sorted_group, flat_group)
    rank = (place_of - first_place).reshape(COLS, N_NARROW, SLOTS)

    def find(partner_rows, query):
        partner_sorted = sorted_group[partner_rows]
        partner_index = sorted_index[partner_rows]
        begin = jax.vmap(lambda edges, target: jnp.searchsorted(edges, target, side='left'))(partner_sorted, query.reshape(device_count, SLOTS))
        wanted = begin + rank.reshape(device_count, SLOTS)
        clipped = jnp.minimum(wanted, SLOTS - 1)
        found = (wanted < SLOTS) & (jnp.take_along_axis(partner_sorted, clipped, axis=1) == query.reshape(device_count, SLOTS))
        partner_slot = jnp.take_along_axis(partner_index, clipped, axis=1)
        return (found.reshape(COLS, N_NARROW, SLOTS), (partner_rows[:, None] * SLOTS + partner_slot).reshape(COLS, N_NARROW, SLOTS))
    row_ids = jnp.arange(device_count)
    col_of_row = row_ids // N_NARROW
    half_of_row = row_ids % N_NARROW
    across_rows = ((col_of_row ^ 1) * N_NARROW + half_of_row).astype(jnp.int32)
    below_rows = (col_of_row * N_NARROW + jnp.minimum(half_of_row + 1, N_NARROW - 1)).astype(jnp.int32)
    found_h, target_h = find(across_rows, group)
    found_same, target_same = find(row_ids.astype(jnp.int32), group + 1)
    found_next, target_next = find(below_rows, (source * TILE_DEV + jnp.zeros_like(group)).astype(jnp.int32))
    at_edge = tile_local == TILE_DEV - 1
    found_v = jnp.where(at_edge, found_next & (half_index + 1 < N_NARROW), found_same)
    target_v = jnp.where(at_edge, target_next, target_same)
    coin = jax.random.randint(coin_key, (COLS, N_NARROW, SLOTS), 0, 10) < 7
    driver_h = active & (rank % 2 == 0) & (col_index % 2 == 0) & found_h & coin
    driver_v = active & (rank % 2 == 1) & (tile_row % 2 == 1) & (tile_row + 1 < ROWS) & found_v & coin
    received_ids = send.reshape(COLS, N_NARROW, COLS, CAP).transpose(2, 1, 0, 3).reshape(COLS, N_NARROW, SLOTS)
    flat_ids = received_ids.reshape(-1)
    total_slots = COLS * N_NARROW * SLOTS
    target = jnp.where(driver_h, target_h, jnp.where(driver_v, target_v, total_slots)).reshape(-1)
    flat_ids = flat_ids.at[target].set(flat_ids, mode='drop')
    new_send = flat_ids.reshape(COLS, N_NARROW, COLS, CAP).transpose(2, 1, 0, 3).reshape(COLS, N_NARROW, SLOTS).astype(jnp.int32)
    border = jnp.where(driver_h, 1, jnp.where(driver_v, 2, 0)).astype(jnp.int32)
    by_source = to_send_layout(tile_row)
    col_source = to_send_layout(jnp.broadcast_to(col_index, (COLS, N_NARROW, SLOTS)))
    border_source = to_send_layout(border)
    inverse = jnp.argsort(send.reshape(COLS, GS_DEV), axis=1, stable=True)
    home_row = jnp.take_along_axis(by_source, inverse, axis=1)
    home_col = jnp.take_along_axis(col_source, inverse, axis=1)
    home_border = jnp.take_along_axis(border_source, inverse, axis=1)
    return (new_send, lists.astype(jnp.int32), lengths.reshape(COLS, ROWS), home_row, home_col, home_border)


def draw_send_slots(key, part):
    return routing(key)[0]


def draw_tile_lists(key, part):
    return routing(key)[1]


def draw_tile_lengths(key, part):
    return routing(key)[2]


def draw_splats(key, part):
    routed = routing(key)
    home_row = routed[3].astype(jnp.float32)
    home_col = routed[4].astype(jnp.float32)
    home_border = routed[5]
    key = jax.random.fold_in(key, 7)
    keys = jax.random.split(key, 10)
    shape = (COLS, GS_DEV)
    inner_x = 16.0 * home_col + jax.random.uniform(keys[0], shape, jnp.float32, 1.0, 15.0)
    inner_y = 16.0 * home_row + jax.random.uniform(keys[1], shape, jnp.float32, 1.0, 15.0)
    edge_x = 16.0 * (home_col + 1.0) + jax.random.uniform(keys[8], shape, jnp.float32, -3.0, 3.0)
    edge_y = 16.0 * (home_row + 1.0) + jax.random.uniform(keys[9], shape, jnp.float32, -3.0, 3.0)
    centre_x = jnp.where(home_border == 1, edge_x, inner_x)
    centre_y = jnp.where(home_border == 2, edge_y, inner_y)
    sigma_x = jnp.exp(jax.random.uniform(keys[2], shape, jnp.float32, math.log(1.5), math.log(5.0)))
    sigma_y = jnp.exp(jax.random.uniform(keys[3], shape, jnp.float32, math.log(1.5), math.log(5.0)))
    tilt = jax.random.uniform(keys[4], shape, jnp.float32, -0.6, 0.6)
    spread = 1.0 - tilt * tilt
    conic_a = 1.0 / (sigma_x * sigma_x * spread)
    conic_b = -tilt / (sigma_x * sigma_y * spread)
    conic_c = 1.0 / (sigma_y * sigma_y * spread)
    logit = jax.random.uniform(keys[5], shape, jnp.float32, -5.0, -1.5)
    colours = jnp.clip(jax.random.normal(keys[7], (CH, COLS, GS_DEV), jnp.float32), -4.0, 4.0)
    head = jnp.stack([centre_x, centre_y, conic_a, conic_b, conic_c, logit], axis=0)
    return jnp.concatenate([head, colours], axis=0).reshape(6 + CH, COLS * GS_DEV)


def steps_of(key, dims, cuts, least, largest):
    loudness = 1.0
    for axis_at, blocks in cuts:
        heights = jax.random.uniform(jax.random.fold_in(jax.random.fold_in(key, 6), axis_at), (blocks,), jnp.float32, least / len(cuts), largest / len(cuts))
        loudness = loudness * jnp.repeat(jnp.exp(heights), dims[axis_at] // blocks).reshape((-1,) + (1,) * (len(dims) - 1 - axis_at))
    return loudness


def gaussian(stream_key, extent, deviation, reach, cuts=(), held_as=jnp.bfloat16):
    values = jax.random.normal(stream_key, extent, jnp.float32) * deviation
    if len(cuts) > 0:
        values = steps_of(stream_key, extent, cuts, -0.22, 0.18) * values
    return jnp.clip(values, min=-reach, max=reach).astype(held_as)


def setup_inputs(seed: int = 0, part: int = 0) -> dict:
    key_list = jax.random.split(jax.random.key(seed), 6)
    part_keys = jax.random.split(jax.random.fold_in(key_list[5], part), 6)
    return {
        "splats": draw_splats(jax.random.fold_in(jax.random.fold_in(key_list[5], part), 71), part),
        "send_slots": draw_send_slots(jax.random.fold_in(jax.random.fold_in(key_list[5], part), 71), part),
        "tile_lists": draw_tile_lists(jax.random.fold_in(jax.random.fold_in(key_list[5], part), 71), part),
        "tile_lengths": draw_tile_lengths(jax.random.fold_in(jax.random.fold_in(key_list[5], part), 71), part),
        "pixel_grads": gaussian(part_keys[4], (CH, COLS, ROWS, PIX), 1.0, 6.0, ((1, 8), (2, 2)), jnp.float32),
    }


def tile_image(params, lengths, starts_x, starts_y):
    list_depth = params.shape[2]
    pixel_index = jnp.arange(256)
    pixel_x = (pixel_index % 16).astype(jnp.float32) + 0.5
    pixel_y = (pixel_index // 16).astype(jnp.float32) + 0.5
    pos_x = (starts_x[:, None] + pixel_x[None, :])[:, None, :]
    pos_y = (starts_y[:, None] + pixel_y[None, :])[:, None, :]
    delta_x = pos_x - params[0][:, :, None]
    delta_y = pos_y - params[1][:, :, None]
    exponent = -0.5 * (params[2][:, :, None] * delta_x * delta_x + params[4][:, :, None] * delta_y * delta_y) - params[3][:, :, None] * delta_x * delta_y
    active_mask = (jnp.arange(list_depth)[None, :] < lengths[:, None]).astype(jnp.float32)
    opacity = jax.nn.sigmoid(params[5]) * active_mask
    alpha_value = opacity[:, :, None] * jnp.exp(exponent)
    log_clear = jnp.log1p(-alpha_value)
    before = jnp.cumsum(log_clear, axis=1) - log_clear
    weight = jnp.exp(before) * alpha_value
    return jnp.einsum('bkp,cbk->cbp', weight, params[6:], precision=lax.Precision.HIGHEST)

def reference(splats, send_slots, tile_lists, tile_lengths, pixel_grads):
    features = splats.shape[0]
    offsets = (jnp.arange(COLS) * GS_DEV).astype(jnp.int32)
    global_sent = send_slots + offsets[:, None, None]
    arrived = global_sent.reshape(COLS, N_NARROW, COLS, CAP).transpose(2, 1, 0, 3).reshape(COLS, N_NARROW, SLOTS)
    halves = (jnp.arange(ROWS) // TILE_DEV).astype(jnp.int32)
    starts_y = (jnp.arange(ROWS) * 16).astype(jnp.float32)

    def column_grads(inputs):
        arrived_col, lists_col, lengths_col, cotangent, col_number = inputs
        splat_ids = arrived_col[halves[:, None], lists_col]
        params = jnp.take(splats, splat_ids.reshape(-1), axis=1).reshape(features, ROWS, K)
        starts_x = jnp.zeros((ROWS,), jnp.float32) + 16.0 * col_number.astype(jnp.float32)
        rendered, pullback = jax.vjp(lambda values: tile_image(values, lengths_col, starts_x, starts_y), params)
        return (pullback(cotangent)[0], splat_ids)
    entry_grads, splat_ids = lax.map(column_grads, (arrived, tile_lists, tile_lengths, jnp.moveaxis(pixel_grads, 1, 0), jnp.arange(COLS).astype(jnp.int32)))
    moved = jnp.moveaxis(entry_grads, 1, 0).reshape(features, -1)
    return jnp.zeros((features, COLS * GS_DEV), jnp.float32).at[:, splat_ids.reshape(-1)].add(moved)
```

```python
import functools
import math

import jax
import jax.numpy as jnp
from jax import lax
from jax.experimental import pallas as pl
from jax.experimental.pallas import tpu as pltpu
from jax.sharding import PartitionSpec as P

LANES = 128
F32 = jnp.float32
BF16 = jnp.bfloat16
LOG2E = math.log2(math.e)
VMEM_BYTES = 48 * 1024 * 1024


def params_of():
    return pltpu.CompilerParams(vmem_limit_bytes=VMEM_BYTES)


def whole(*_):
    return pl.BlockSpec(memory_space=pltpu.VMEM)


def split2(values):
    high = values.astype(BF16)
    low = (values - high.astype(F32)).astype(BF16)
    return high, low


def split3(values):
    high = values.astype(BF16)
    rest = values - high.astype(F32)
    middle = rest.astype(BF16)
    low = (rest - middle.astype(F32)).astype(BF16)
    return high, middle, low


def gather_lanes(index_row, load_chunk, chunk_count):
    index = jnp.broadcast_to(index_row, (8, LANES))
    lane = index & (LANES - 1)
    chunk = index >> 7
    top = jnp.zeros((8, LANES), F32)
    bottom = jnp.zeros((8, LANES), F32)
    for c in range(chunk_count):
        block = load_chunk(c)
        here = chunk == c
        top = jnp.where(
            here, jnp.take_along_axis(block[:8], lane, axis=1, mode="promise_in_bounds"), top
        )
        bottom = jnp.where(
            here, jnp.take_along_axis(block[8:], lane, axis=1, mode="promise_in_bounds"), bottom
        )
    return jnp.concatenate([top, bottom], axis=0)


def send_kernel(index_ref, source_ref, out_ref):
    per = out_ref.shape[2] // LANES
    chunk_count = source_ref.shape[1] // LANES

    def step(j, carry):
        rows = gather_lanes(
            index_ref[pl.ds(j, 1), :],
            lambda c: source_ref[:, c * LANES : (c + 1) * LANES],
            chunk_count,
        )
        place = pl.multiple_of((j % per) * LANES, LANES)
        out_ref[j // per, :, pl.ds(place, LANES)] = rows
        return carry

    lax.fori_loop(0, index_ref.shape[0], step, 0)


def entry_kernel(index_ref, source_ref, out_ref):
    per = source_ref.shape[2] // LANES
    chunk_count = source_ref.shape[0] * per

    def step(j, carry):
        rows = gather_lanes(
            index_ref[pl.ds(j, 1), :],
            lambda c: source_ref[c // per, :, (c % per) * LANES : (c % per + 1) * LANES],
            chunk_count,
        )
        out_ref[:, pl.ds(pl.multiple_of(j * LANES, LANES), LANES)] = rows
        return carry

    lax.fori_loop(0, index_ref.shape[0], step, 0)


def one_tile(params, grads, length, centre_x, centre_y, before_ones, after_ones, moments):
    depth = params.shape[1]
    side = 16
    u = params[0:1] - centre_x
    v = params[1:2] - centre_y
    a = params[2:3]
    b = params[3:4]
    c = params[4:5]
    logit = params[5:6]
    local = lax.broadcasted_iota(jnp.int32, (side, depth), 0).astype(F32) - 7.5
    dx = local - u
    dy = local - v
    live = lax.broadcasted_iota(jnp.int32, (1, depth), 1) < length
    log_opacity = -(jnp.maximum(-logit, 0.0) + jnp.log(1.0 + jnp.exp(-jnp.abs(logit))))
    log_opacity = jnp.where(live, log_opacity * LOG2E, -1e30)
    part_x = (-0.5 * LOG2E) * (a * dx * dx)
    part_y = (-0.5 * LOG2E) * (c * dy * dy) + log_opacity
    cross = LOG2E * (b * dx)
    exponent = (part_x[None] + part_y[:, None]) - cross[None] * dy[:, None]
    exponent = exponent.reshape(side * side, depth)
    alpha = jnp.exp2(exponent)
    log_clear = jnp.log(1.0 - alpha) * LOG2E
    clear_high, clear_low = split2(log_clear)
    before = jnp.dot(clear_high, before_ones, preferred_element_type=F32) + jnp.dot(
        clear_low, before_ones, preferred_element_type=F32
    )
    weight = jnp.exp2(before) * alpha
    ratio = jnp.exp2(exponent - log_clear)
    grads_high, grads_low = split2(grads)
    colour_high, colour_low = split2(params[6:])
    pulled = lax.dot_general(
        jnp.concatenate([grads_high, grads_low, grads_high], axis=0),
        jnp.concatenate([colour_high, colour_high, colour_low], axis=0),
        (((0,), (0,)), ((), ())),
        preferred_element_type=F32,
    )
    flow = weight * pulled
    flow_high, flow_low = split2(flow)
    after = jnp.dot(flow_high, after_ones, preferred_element_type=F32) + jnp.dot(
        flow_low, after_ones, preferred_element_type=F32
    )
    change = flow - after * ratio
    weight_high, weight_low = split2(weight)
    colour_grads = (
        jnp.dot(grads_high, weight_high, preferred_element_type=F32)
        + jnp.dot(grads_low, weight_high, preferred_element_type=F32)
        + jnp.dot(grads_high, weight_low, preferred_element_type=F32)
    )
    sums = sum(jnp.dot(moments, piece, preferred_element_type=F32) for piece in split3(change))
    m00, m10, m01, m20, m02, m11 = (sums[i : i + 1] for i in range(6))
    sx = m10 - u * m00
    sy = m01 - v * m00
    sxx = m20 - 2.0 * u * m10 + u * u * m00
    syy = m02 - 2.0 * v * m01 + v * v * m00
    sxy = m11 - u * m01 - v * m10 + u * v * m00
    closed = 1.0 / (1.0 + jnp.exp(logit))
    return jnp.concatenate(
        [
            a * sx + b * sy,
            c * sy + b * sx,
            -0.5 * sxx,
            -sxy,
            -0.5 * syy,
            m00 * closed,
            colour_grads,
        ],
        axis=0,
    )


def tile_kernel(per_step, length_ref, params_ref, grads_ref, out_ref):
    depth = out_ref.shape[1] // per_step
    first = pl.program_id(0) * per_step
    row_base = lax.axis_index("narrow") * (pl.num_programs(0) * per_step)
    centre_x = (lax.axis_index("wide") * 16 + 8).astype(F32)
    low = lax.broadcasted_iota(jnp.int32, (depth, depth), 0)
    high = lax.broadcasted_iota(jnp.int32, (depth, depth), 1)
    before_ones = (low < high).astype(F32).astype(BF16)
    after_ones = (low > high).astype(F32).astype(BF16)
    pixel = lax.broadcasted_iota(jnp.int32, (8, 256), 1)
    which = lax.broadcasted_iota(jnp.int32, (8, 256), 0)
    x = (pixel & 15).astype(F32) - 7.5
    y = (pixel >> 4).astype(F32) - 7.5
    moments = jnp.where(which == 0, 1.0, 0.0)
    for i, term in enumerate((x, y, x * x, y * y, x * y)):
        moments = jnp.where(which == i + 1, term, moments)
    moments = moments.astype(BF16)
    for i in range(per_step):
        centre_y = ((row_base + first + i) * 16 + 8).astype(F32)
        out_ref[:, i * depth : (i + 1) * depth] = one_tile(
            params_ref[:, i * depth : (i + 1) * depth],
            grads_ref[i],
            length_ref[first + i],
            centre_x,
            centre_y,
            before_ones,
            after_ones,
            moments,
        )


GROUP = 16
STRIP = 256
ENTRY_BLOCK = 2048


def scatter_group(group, index_ref, load_values, out_store, spread_ref):
    entry_count = index_ref.shape[1]
    total = jnp.zeros((GROUP * 32, STRIP), F32)
    column = lax.broadcasted_iota(jnp.int32, (STRIP, ENTRY_BLOCK), 0)
    for block in range(entry_count // ENTRY_BLOCK):
        start = block * ENTRY_BLOCK
        index = index_ref[:, start : start + ENTRY_BLOCK]
        strip = index >> 8
        hot = jnp.where(column == (index & (STRIP - 1)), 1.0, 0.0).astype(BF16)
        high, low = split2(load_values(start))
        both = jnp.concatenate([high, low], axis=0)
        for c in range(GROUP):
            mask = jnp.where(strip == group * GROUP + c, 1.0, 0.0).astype(BF16)
            spread_ref[c * 32 : (c + 1) * 32, :] = both * mask
        total += lax.dot_general(
            spread_ref[...], hot, (((1,), (1,)), ((), ())), preferred_element_type=F32
        )
    for c in range(GROUP):
        out_store(c, total[c * 32 : c * 32 + 16] + total[c * 32 + 16 : c * 32 + 32])


def slot_kernel(index_ref, value_ref, out_ref, spread_ref):
    per = out_ref.shape[2] // LANES

    def store(group, c, rows):
        for part in range(STRIP // LANES):
            chunk = (group * GROUP + c) * (STRIP // LANES) + part
            place = (chunk % per) * LANES
            out_ref[chunk // per, :, place : place + LANES] = rows[
                :, part * LANES : (part + 1) * LANES
            ]

    strips = out_ref.shape[0] * out_ref.shape[2] // STRIP
    for group in range(strips // GROUP):
        scatter_group(
            group,
            index_ref,
            lambda start: value_ref[:, start : start + ENTRY_BLOCK],
            functools.partial(store, group),
            spread_ref,
        )


def splat_kernel(index_ref, value_ref, out_ref, spread_ref):
    cap = value_ref.shape[2]

    def load(start):
        if cap >= ENTRY_BLOCK:
            place = start % cap
            return value_ref[start // cap, :, place : place + ENTRY_BLOCK]
        return jnp.concatenate(
            [value_ref[start // cap + i] for i in range(ENTRY_BLOCK // cap)], axis=1
        )

    def store(c, rows):
        out_ref[:, c * STRIP : (c + 1) * STRIP] = rows

    scatter_group(pl.program_id(0), index_ref, load, store, spread_ref)


def body(splats, send_slots, tile_lists, tile_lengths, pixel_grads):
    features, local_count = splats.shape
    slot_count = send_slots.shape[2]
    tile_count, depth = tile_lists.shape[1:]
    entry_count = tile_count * depth
    columns = lax.axis_size("wide")
    cap = slot_count // columns
    sent_index = send_slots.reshape(slot_count // LANES, LANES)
    outgoing = pl.pallas_call(
        send_kernel,
        out_shape=jax.ShapeDtypeStruct((columns, features, cap), F32),
        in_specs=[whole(), whole()],
        out_specs=whole(),
        compiler_params=params_of(),
        name="send_gather",
    )(sent_index, splats)
    received = lax.all_to_all(outgoing, "wide", split_axis=0, concat_axis=0, tiled=True)
    all_params = pl.pallas_call(
        entry_kernel,
        out_shape=jax.ShapeDtypeStruct((features, entry_count), F32),
        in_specs=[whole(), whole()],
        out_specs=whole(),
        compiler_params=params_of(),
        name="entry_gather",
    )(tile_lists.reshape(entry_count // LANES, LANES), received)
    per_step = 2
    channels, pixels = pixel_grads.shape[0], pixel_grads.shape[3]
    grads_here = jnp.moveaxis(pixel_grads[:, 0], 1, 0)
    entry_grads = pl.pallas_call(
        functools.partial(tile_kernel, per_step),
        out_shape=jax.ShapeDtypeStruct((features, entry_count), F32),
        grid=(tile_count // per_step,),
        in_specs=[
            pl.BlockSpec(memory_space=pltpu.SMEM),
            pl.BlockSpec((features, per_step * depth), lambda i: (0, i)),
            pl.BlockSpec((per_step, channels, pixels), lambda i: (i, 0, 0)),
        ],
        out_specs=pl.BlockSpec((features, per_step * depth), lambda i: (0, i)),
        compiler_params=params_of(),
        name="tile_grads",
    )(tile_lengths.reshape(tile_count), all_params, grads_here)
    spread = pltpu.VMEM((GROUP * 32, ENTRY_BLOCK), BF16)
    slot_grads = pl.pallas_call(
        slot_kernel,
        out_shape=jax.ShapeDtypeStruct((columns, features, cap), F32),
        in_specs=[whole(), whole()],
        out_specs=whole(),
        scratch_shapes=[spread],
        compiler_params=params_of(),
        name="slot_scatter",
    )(tile_lists.reshape(1, entry_count), entry_grads)
    returned = lax.all_to_all(slot_grads, "wide", split_axis=0, concat_axis=0, tiled=True)
    partial_grads = pl.pallas_call(
        splat_kernel,
        out_shape=jax.ShapeDtypeStruct((features, local_count), F32),
        grid=(local_count // (GROUP * STRIP),),
        in_specs=[
            pl.BlockSpec((1, slot_count), lambda i: (0, 0)),
            pl.BlockSpec((columns, features, cap), lambda i: (0, 0, 0)),
        ],
        out_specs=pl.BlockSpec((features, GROUP * STRIP), lambda i: (0, i)),
        scratch_shapes=[spread],
        compiler_params=params_of(),
        name="splat_scatter",
    )(send_slots.reshape(1, slot_count), returned)
    other = lax.ppermute(partial_grads, "narrow", [(0, 1), (1, 0)])
    return partial_grads + other


def solution(mesh):
    placed = (
        P(None, ("groups", "wide")),
        P(("groups", "wide"), "narrow", None),
        P(("groups", "wide"), "narrow", None),
        P(("groups", "wide"), "narrow"),
        P(None, ("groups", "wide"), "narrow", None),
    )
    return jax.shard_map(
        body, mesh=mesh, in_specs=placed, out_specs=P(None, ("groups", "wide")), check_vma=False
    )
```

```python
import functools
import math

import jax
import jax.numpy as jnp
from jax import lax
from jax.experimental import pallas as pl
from jax.experimental.pallas import tpu as pltpu
from jax.sharding import PartitionSpec as P

LANES = 128
F32 = jnp.float32
BF16 = jnp.bfloat16
LOG2E = math.log2(math.e)
VMEM_BYTES = 48 * 1024 * 1024


def params_of():
    return pltpu.CompilerParams(vmem_limit_bytes=VMEM_BYTES)


def whole(*_):
    return pl.BlockSpec(memory_space=pltpu.VMEM)


def split2(values):
    high = values.astype(BF16)
    low = (values - high.astype(F32)).astype(BF16)
    return high, low


def split3(values):
    high = values.astype(BF16)
    rest = values - high.astype(F32)
    middle = rest.astype(BF16)
    low = (rest - middle.astype(F32)).astype(BF16)
    return high, middle, low


STRIP = 256
PAIR_ROWS = 80
PAIRS_PER_DOT = 8
MESH = pl.DeviceIdType.MESH


def spread_pair(first_strip, second_strip):
    first = split3(first_strip)
    second = split3(second_strip)
    low = jnp.concatenate([first[2].astype(F32)[:8], second[2].astype(F32)[:8]], axis=0)
    return jnp.concatenate([first[0], first[1], second[0], second[1], low.astype(BF16)], axis=0)


def gather_strip(index, spread_ref, first_pair, pair_count, strip_of):
    width = spread_ref.shape[1]
    count = index.shape[1]
    strip = jnp.broadcast_to(index // width, (8, count))
    column = lax.broadcasted_iota(jnp.int32, (width, count), 0)
    hot = jnp.where(column == (index & (width - 1)), 1.0, 0.0).astype(BF16)
    parts = [jnp.zeros((8, count), F32) for _ in range(5)]
    per_dot = min(PAIRS_PER_DOT, pair_count)
    rows = per_dot * PAIR_ROWS
    for block in range(pair_count // per_dot):
        start_row = first_pair * PAIR_ROWS + block * rows
        found = jnp.dot(
            spread_ref[start_row : start_row + rows, :], hot, preferred_element_type=F32
        )
        for p in range(per_dot):
            for q in range(2):
                here = strip == strip_of((first_pair + block * per_dot + p) * 2 + q)
                base = p * PAIR_ROWS
                starts = [base + q * 32 + 8 * i for i in range(4)] + [base + 64 + 8 * q]
                parts = [
                    jnp.where(here, found[start : start + 8], part)
                    for start, part in zip(starts, parts)
                ]
    return jnp.concatenate([parts[0] + (parts[2] + parts[4]), parts[1] + parts[3]], axis=0)


def copy_between(send_ref, recv_ref, send_sems, recv_sems, peer, mine):
    return pltpu.make_async_remote_copy(
        src_ref=send_ref.at[peer],
        dst_ref=recv_ref.at[mine],
        send_sem=send_sems.at[peer],
        recv_sem=recv_sems.at[mine],
        device_id={"wide": peer},
        device_id_type=MESH,
    )


def greet(columns, me):
    barrier = pltpu.get_barrier_semaphore()

    def hello(step, carry):
        peer = lax.rem(me + 1 + step, columns)
        pl.semaphore_signal(barrier, inc=1, device_id={"wide": peer}, device_id_type=MESH)
        return carry

    lax.fori_loop(0, columns - 1, hello, 0)
    return barrier


def wait_sends(columns, me, send_ref, recv_ref, send_sems, recv_sems):
    def done(step, carry):
        peer = lax.rem(me + 1 + step, columns)
        copy_between(send_ref, recv_ref, send_sems, recv_sems, peer, me).wait_send()
        return carry

    lax.fori_loop(0, columns - 1, done, 0)


def offset_of(step, columns):
    away = (step + 1) // 2
    return columns // 2 + away * (1 - 2 * (step % 2))


def receive_kernel(
    sent_ref, source_ref, list_ref, out_ref,
    spread_ref, spread_recv_ref, send_ref, recv_ref, send_sems, recv_sems,
):
    columns, _, cap = recv_ref.shape
    me = lax.axis_index("wide")
    barrier = greet(columns, me)
    source_strips = source_ref.shape[1] // STRIP
    for p in range(source_strips // 2):
        start = p * 2 * STRIP
        spread_ref[p * PAIR_ROWS : (p + 1) * PAIR_ROWS, :] = spread_pair(
            source_ref[:, start : start + STRIP], source_ref[:, start + STRIP : start + 2 * STRIP]
        )
    pl.semaphore_wait(barrier, columns - 1)
    width = sent_ref.shape[1]
    per = cap // width

    def pick(peer, place):
        index = sent_ref[pl.ds(peer * per + place, 1), :]
        return gather_strip(index, spread_ref, 0, source_strips // 2, lambda strip: strip)

    def send(step, carry):
        peer = lax.rem(me + offset_of(step, columns), columns)
        for i in range(per):
            send_ref[peer, :, i * width : (i + 1) * width] = pick(peer, i)
        copy_between(send_ref, recv_ref, send_sems, recv_sems, peer, me).start()
        return carry

    lax.fori_loop(0, columns - 1, send, 0)
    for i in range(per):
        recv_ref[me, :, i * width : (i + 1) * width] = pick(me, i)

    half = columns // 2
    strips_half = half * per
    pairs_half = strips_half // 2
    sources = [lax.rem(me + columns - offset_of(k, columns), columns) for k in range(columns)]
    for phase in range(2):
        for k in range(phase * half, (phase + 1) * half):
            if k < columns - 1:
                copy_between(send_ref, recv_ref, send_sems, recv_sems, sources[k], sources[k]).wait_recv()
        strips = [
            (sources[phase * half + i // per], (i % per) * width) for i in range(strips_half)
        ]
        for p in range(pairs_half):
            blocks = [
                recv_ref[source, :, place : place + width]
                for source, place in strips[2 * p : 2 * p + 2]
            ]
            row = (phase * pairs_half + p) * PAIR_ROWS
            spread_recv_ref[row : row + PAIR_ROWS, :] = spread_pair(*blocks)

        def step(j, carry):
            found = gather_strip(
                list_ref[pl.ds(j, 1), :],
                spread_recv_ref,
                phase * pairs_half,
                pairs_half,
                lambda strip: sources[strip // per] * per + strip % per,
            )
            where = pl.ds(pl.multiple_of(j * STRIP, STRIP), STRIP)
            out_ref[:, where] = found if phase == 0 else out_ref[:, where] + found
            return carry

        lax.fori_loop(0, list_ref.shape[0], step, 0, unroll=2)
    wait_sends(columns, me, send_ref, recv_ref, send_sems, recv_sems)


def one_tile(params, grads, length, centre_x, centre_y, before_ones, after_ones, moments):
    depth = params.shape[1]
    side = 16
    u = params[0:1] - centre_x
    v = params[1:2] - centre_y
    a = params[2:3]
    b = params[3:4]
    c = params[4:5]
    logit = params[5:6]
    local = lax.broadcasted_iota(jnp.int32, (side, depth), 0).astype(F32) - 7.5
    dx = local - u
    dy = local - v
    live = lax.broadcasted_iota(jnp.int32, (1, depth), 1) < length
    log_opacity = -(jnp.maximum(-logit, 0.0) + jnp.log(1.0 + jnp.exp(-jnp.abs(logit))))
    log_opacity = jnp.where(live, log_opacity * LOG2E, -1e30)
    part_x = (-0.5 * LOG2E) * (a * dx * dx)
    part_y = (-0.5 * LOG2E) * (c * dy * dy) + log_opacity
    cross = LOG2E * (b * dx)
    exponent = (part_x[None] + part_y[:, None]) - cross[None] * dy[:, None]
    exponent = exponent.reshape(side * side, depth)
    alpha = jnp.exp2(exponent)
    log_clear = jnp.log(1.0 - alpha) * LOG2E
    clear_high, clear_low = split2(log_clear)
    before = jnp.dot(clear_high, before_ones, preferred_element_type=F32) + jnp.dot(
        clear_low, before_ones, preferred_element_type=F32
    )
    weight = jnp.exp2(before) * alpha
    ratio = jnp.exp2(exponent - log_clear)
    grads_high, grads_low = split2(grads)
    colour_high, colour_low = split2(params[6:])
    pulled = lax.dot_general(
        jnp.concatenate([grads_high, grads_low, grads_high], axis=0),
        jnp.concatenate([colour_high, colour_high, colour_low], axis=0),
        (((0,), (0,)), ((), ())),
        preferred_element_type=F32,
    )
    flow = weight * pulled
    flow_high, flow_low = split2(flow)
    after = jnp.dot(flow_high, after_ones, preferred_element_type=F32) + jnp.dot(
        flow_low, after_ones, preferred_element_type=F32
    )
    change = flow - after * ratio
    weight_high, weight_low = split2(weight)
    colour_grads = (
        jnp.dot(grads_high, weight_high, preferred_element_type=F32)
        + jnp.dot(grads_low, weight_high, preferred_element_type=F32)
        + jnp.dot(grads_high, weight_low, preferred_element_type=F32)
    )
    sums = sum(jnp.dot(moments, piece, preferred_element_type=F32) for piece in split3(change))
    m00, m10, m01, m20, m02, m11 = (sums[i : i + 1] for i in range(6))
    sx = m10 - u * m00
    sy = m01 - v * m00
    sxx = m20 - 2.0 * u * m10 + u * u * m00
    syy = m02 - 2.0 * v * m01 + v * v * m00
    sxy = m11 - u * m01 - v * m10 + u * v * m00
    closed = 1.0 / (1.0 + jnp.exp(logit))
    return jnp.concatenate(
        [
            a * sx + b * sy,
            c * sy + b * sx,
            -0.5 * sxx,
            -sxy,
            -0.5 * syy,
            m00 * closed,
            colour_grads,
        ],
        axis=0,
    )


def tile_kernel(per_step, length_ref, params_ref, grads_ref, out_ref):
    depth = out_ref.shape[1] // per_step
    first = pl.program_id(0) * per_step
    row_base = lax.axis_index("narrow") * (pl.num_programs(0) * per_step)
    centre_x = (lax.axis_index("wide") * 16 + 8).astype(F32)
    low = lax.broadcasted_iota(jnp.int32, (depth, depth), 0)
    high = lax.broadcasted_iota(jnp.int32, (depth, depth), 1)
    before_ones = (low < high).astype(F32).astype(BF16)
    after_ones = (low > high).astype(F32).astype(BF16)
    pixel = lax.broadcasted_iota(jnp.int32, (8, 256), 1)
    which = lax.broadcasted_iota(jnp.int32, (8, 256), 0)
    x = (pixel & 15).astype(F32) - 7.5
    y = (pixel >> 4).astype(F32) - 7.5
    moments = jnp.where(which == 0, 1.0, 0.0)
    for i, term in enumerate((x, y, x * x, y * y, x * y)):
        moments = jnp.where(which == i + 1, term, moments)
    moments = moments.astype(BF16)
    for i in range(per_step):
        centre_y = ((row_base + first + i) * 16 + 8).astype(F32)
        out_ref[:, i * depth : (i + 1) * depth] = one_tile(
            params_ref[:, i * depth : (i + 1) * depth],
            grads_ref[i],
            length_ref[first + i],
            centre_x,
            centre_y,
            before_ones,
            after_ones,
            moments,
        )


GROUP = 16
ENTRY_BLOCK = 2048


def scatter_group(group, blocks, spread_ref):
    total = jnp.zeros((GROUP * 32, STRIP), F32)
    column = lax.broadcasted_iota(jnp.int32, (STRIP, ENTRY_BLOCK), 0)
    for load_index, load_values in blocks:
        index = load_index()
        strip = index >> 8
        hot = jnp.where(column == (index & (STRIP - 1)), 1.0, 0.0).astype(BF16)
        high, low = split2(load_values())
        both = jnp.concatenate([high, low], axis=0)
        for c in range(GROUP):
            mask = jnp.where(strip == group * GROUP + c, 1.0, 0.0).astype(BF16)
            spread_ref[c * 32 : (c + 1) * 32, :] = both * mask
        total += lax.dot_general(
            spread_ref[...], hot, (((1,), (1,)), ((), ())), preferred_element_type=F32
        )
    return [
        total[c * 32 : c * 32 + 16] + total[c * 32 + 16 : c * 32 + 32] for c in range(GROUP)
    ]


def return_kernel(
    list_ref, value_ref, sent_ref, out_ref, spread_ref, send_ref, recv_ref, send_sems, recv_sems
):
    columns, _, cap = recv_ref.shape
    me = lax.axis_index("wide")
    barrier = greet(columns, me)
    half = columns // 2
    my_half = me // half
    entry_blocks = [
        (
            lambda start=start: list_ref[:, start : start + ENTRY_BLOCK],
            lambda start=start: value_ref[:, start : start + ENTRY_BLOCK],
        )
        for start in range(0, list_ref.shape[1], ENTRY_BLOCK)
    ]
    for phase in range(2):
        group = my_half if phase else 1 - my_half
        strips = scatter_group(group, entry_blocks, spread_ref)
        for c, rows in enumerate(strips):
            for part in range(STRIP // LANES):
                start = c * STRIP + part * LANES
                place = start % cap
                send_ref[group * half + start // cap, :, place : place + LANES] = rows[
                    :, part * LANES : (part + 1) * LANES
                ]
        if phase == 0:
            pl.semaphore_wait(barrier, columns - 1)

        def send(step, carry):
            peer = group * half + lax.rem(me + step, half)
            copy_between(send_ref, recv_ref, send_sems, recv_sems, peer, me).start()
            return carry

        lax.fori_loop(phase, half, send, 0)
    recv_ref[me] = send_ref[me]

    per_block = ENTRY_BLOCK // cap
    for phase in range(2):
        from_half = my_half if phase else 1 - my_half

        def arrived(step, carry):
            source = from_half * half + lax.rem(me + step, half)
            copy_between(send_ref, recv_ref, send_sems, recv_sems, source, source).wait_recv()
            return carry

        lax.fori_loop(phase, half, arrived, 0)
        blocks = []
        for block in range(half // per_block):
            first = from_half * half + block * per_block
            blocks.append(
                (
                    lambda first=first: sent_ref[
                        :, pl.ds(pl.multiple_of(first * cap, LANES), ENTRY_BLOCK)
                    ],
                    lambda first=first: jnp.concatenate(
                        [recv_ref[first + i] for i in range(per_block)], axis=1
                    ),
                )
            )

        def splat_group(group, carry):
            found = scatter_group(group, blocks, spread_ref)
            for c, rows in enumerate(found):
                where = pl.ds(pl.multiple_of((group * GROUP + c) * STRIP, STRIP), STRIP)
                out_ref[:, where] = rows if phase == 0 else out_ref[:, where] + rows
            return carry

        lax.fori_loop(0, out_ref.shape[1] // (GROUP * STRIP), splat_group, 0)
    wait_sends(columns, me, send_ref, recv_ref, send_sems, recv_sems)


def body(splats, send_slots, tile_lists, tile_lengths, pixel_grads):
    features, local_count = splats.shape
    slot_count = send_slots.shape[2]
    tile_count, depth = tile_lists.shape[1:]
    entry_count = tile_count * depth
    columns = lax.axis_size("wide")
    cap = slot_count // columns
    width = min(cap, STRIP)
    exchange = [
        pltpu.VMEM((columns, features, cap), F32),
        pltpu.VMEM((columns, features, cap), F32),
        pltpu.SemaphoreType.DMA((columns,)),
        pltpu.SemaphoreType.DMA((columns,)),
    ]
    all_params = pl.pallas_call(
        receive_kernel,
        out_shape=jax.ShapeDtypeStruct((features, entry_count), F32),
        in_specs=[whole(), whole(), whole()],
        out_specs=whole(),
        scratch_shapes=[
            pltpu.VMEM((local_count // STRIP // 2 * PAIR_ROWS, STRIP), BF16),
            pltpu.VMEM((slot_count // width // 2 * PAIR_ROWS, width), BF16),
        ]
        + exchange,
        compiler_params=pltpu.CompilerParams(
            vmem_limit_bytes=VMEM_BYTES, collective_id=0, has_side_effects=True
        ),
        name="receive_entries",
    )(
        send_slots.reshape(slot_count // width, width),
        splats,
        tile_lists.reshape(entry_count // STRIP, STRIP),
    )
    per_step = 2
    channels, pixels = pixel_grads.shape[0], pixel_grads.shape[3]
    grads_here = jnp.moveaxis(pixel_grads[:, 0], 1, 0)
    entry_grads = pl.pallas_call(
        functools.partial(tile_kernel, per_step),
        out_shape=jax.ShapeDtypeStruct((features, entry_count), F32),
        grid=(tile_count // per_step,),
        in_specs=[
            pl.BlockSpec(memory_space=pltpu.SMEM),
            pl.BlockSpec((features, per_step * depth), lambda i: (0, i)),
            pl.BlockSpec((per_step, channels, pixels), lambda i: (i, 0, 0)),
        ],
        out_specs=pl.BlockSpec((features, per_step * depth), lambda i: (0, i)),
        compiler_params=params_of(),
        name="tile_grads",
    )(tile_lengths.reshape(tile_count), all_params, grads_here)
    partial_grads = pl.pallas_call(
        return_kernel,
        out_shape=jax.ShapeDtypeStruct((features, local_count), F32),
        in_specs=[whole(), whole(), whole()],
        out_specs=whole(),
        scratch_shapes=[pltpu.VMEM((GROUP * 32, ENTRY_BLOCK), BF16)] + exchange,
        compiler_params=pltpu.CompilerParams(
            vmem_limit_bytes=VMEM_BYTES, collective_id=1, has_side_effects=True
        ),
        name="return_grads",
    )(
        tile_lists.reshape(1, entry_count),
        entry_grads,
        send_slots.reshape(1, slot_count),
    )
    other = lax.ppermute(partial_grads, "narrow", [(0, 1), (1, 0)])
    return partial_grads + other


def solution(mesh):
    placed = (
        P(None, ("groups", "wide")),
        P(("groups", "wide"), "narrow", None),
        P(("groups", "wide"), "narrow", None),
        P(("groups", "wide"), "narrow"),
        P(None, ("groups", "wide"), "narrow", None),
    )
    return jax.shard_map(
        body, mesh=mesh, in_specs=placed, out_specs=P(None, ("groups", "wide")), check_vma=False
    )
```

```python
import functools
import math

import jax
import jax.numpy as jnp
from jax import lax
from jax.experimental import pallas as pl
from jax.experimental.pallas import tpu as pltpu
from jax.sharding import PartitionSpec as P

LANES = 128
F32 = jnp.float32
BF16 = jnp.bfloat16
LOG2E = math.log2(math.e)
VMEM_BYTES = 48 * 1024 * 1024


def params_of():
    return pltpu.CompilerParams(vmem_limit_bytes=VMEM_BYTES)


def whole(*_):
    return pl.BlockSpec(memory_space=pltpu.VMEM)


def split2(values):
    high = values.astype(BF16)
    low = (values - high.astype(F32)).astype(BF16)
    return high, low


def split3(values):
    high = values.astype(BF16)
    rest = values - high.astype(F32)
    middle = rest.astype(BF16)
    low = (rest - middle.astype(F32)).astype(BF16)
    return high, middle, low


STRIP = 256
PAIR_ROWS = 80
PAIRS_PER_DOT = 2
MESH = pl.DeviceIdType.MESH


def spread_pair(first_strip, second_strip):
    first = split3(first_strip)
    second = split3(second_strip)
    low = jnp.concatenate([first[2].astype(F32)[:8], second[2].astype(F32)[:8]], axis=0)
    return jnp.concatenate([first[0], first[1], second[0], second[1], low.astype(BF16)], axis=0)


def gather_strip(index, spread_ref, first_pair, pair_count, strip_of):
    width = spread_ref.shape[1]
    count = index.shape[1]
    strip = jnp.broadcast_to(index // width, (8, count))
    column = lax.broadcasted_iota(jnp.int32, (width, count), 0)
    hot = jnp.where(column == (index & (width - 1)), 1.0, 0.0).astype(BF16)
    parts = [jnp.zeros((8, count), F32) for _ in range(5)]
    per_dot = min(PAIRS_PER_DOT, pair_count)
    rows = per_dot * PAIR_ROWS
    for block in range(pair_count // per_dot):
        start_row = first_pair * PAIR_ROWS + block * rows
        found = jnp.dot(
            spread_ref[start_row : start_row + rows, :], hot, preferred_element_type=F32
        )
        for p in range(per_dot):
            for q in range(2):
                here = strip == strip_of((first_pair + block * per_dot + p) * 2 + q)
                base = p * PAIR_ROWS
                starts = [base + q * 32 + 8 * i for i in range(4)] + [base + 64 + 8 * q]
                parts = [
                    jnp.where(here, found[start : start + 8], part)
                    for start, part in zip(starts, parts)
                ]
    return jnp.concatenate([parts[0] + (parts[2] + parts[4]), parts[1] + parts[3]], axis=0)


def copy_between(send_ref, recv_ref, send_sems, recv_sems, peer, mine):
    return pltpu.make_async_remote_copy(
        src_ref=send_ref.at[peer],
        dst_ref=recv_ref.at[mine],
        send_sem=send_sems.at[peer],
        recv_sem=recv_sems.at[mine],
        device_id={"wide": peer},
        device_id_type=MESH,
    )


def greet(columns, me):
    barrier = pltpu.get_barrier_semaphore()

    def hello(step, carry):
        peer = lax.rem(me + 1 + step, columns)
        pl.semaphore_signal(barrier, inc=1, device_id={"wide": peer}, device_id_type=MESH)
        return carry

    lax.fori_loop(0, columns - 1, hello, 0)
    return barrier


def wait_sends(columns, me, send_ref, recv_ref, send_sems, recv_sems):
    def done(step, carry):
        peer = lax.rem(me + 1 + step, columns)
        copy_between(send_ref, recv_ref, send_sems, recv_sems, peer, me).wait_send()
        return carry

    lax.fori_loop(0, columns - 1, done, 0)


def offset_of(step, columns):
    away = (step + 1) // 2
    return columns // 2 + away * (1 - 2 * (step % 2))


def receive_kernel(
    sent_ref, source_ref, list_ref, out_ref,
    spread_ref, spread_recv_ref, send_ref, recv_ref, send_sems, recv_sems,
):
    columns, _, cap = recv_ref.shape
    me = lax.axis_index("wide")
    barrier = greet(columns, me)
    source_strips = source_ref.shape[1] // STRIP
    for p in range(source_strips // 2):
        start = p * 2 * STRIP
        spread_ref[p * PAIR_ROWS : (p + 1) * PAIR_ROWS, :] = spread_pair(
            source_ref[:, start : start + STRIP], source_ref[:, start + STRIP : start + 2 * STRIP]
        )
    pl.semaphore_wait(barrier, columns - 1)
    width = min(cap, STRIP)
    per = cap // width

    def pick(peer, place):
        start = pl.multiple_of((peer * per + place) * width, width)
        index = sent_ref[0, :, pl.ds(start, width)]
        return gather_strip(index, spread_ref, 0, source_strips // 2, lambda strip: strip)

    def send(step, carry):
        peer = lax.rem(me + offset_of(step, columns), columns)
        for i in range(per):
            send_ref[peer, :, i * width : (i + 1) * width] = pick(peer, i)
        copy_between(send_ref, recv_ref, send_sems, recv_sems, peer, me).start()
        return carry

    lax.fori_loop(0, columns - 1, send, 0)
    for i in range(per):
        recv_ref[me, :, i * width : (i + 1) * width] = pick(me, i)

    half = columns // 2
    strips_half = half * per
    pairs_half = strips_half // 2
    sources = [lax.rem(me + columns - offset_of(k, columns), columns) for k in range(columns)]
    for phase in range(2):
        for k in range(phase * half, (phase + 1) * half):
            if k < columns - 1:
                copy_between(send_ref, recv_ref, send_sems, recv_sems, sources[k], sources[k]).wait_recv()
        strips = [
            (sources[phase * half + i // per], (i % per) * width) for i in range(strips_half)
        ]
        for p in range(pairs_half):
            blocks = [
                recv_ref[source, :, place : place + width]
                for source, place in strips[2 * p : 2 * p + 2]
            ]
            row = (phase * pairs_half + p) * PAIR_ROWS
            spread_recv_ref[row : row + PAIR_ROWS, :] = spread_pair(*blocks)

        def step(j, carry):
            found = gather_strip(
                list_ref[0, pl.ds(j, 1), :],
                spread_recv_ref,
                phase * pairs_half,
                pairs_half,
                lambda strip: sources[strip // per] * per + strip % per,
            )
            where = pl.ds(pl.multiple_of(j * STRIP, STRIP), STRIP)
            out_ref[:, where] = found if phase == 0 else out_ref[:, where] + found
            return carry

        lax.fori_loop(0, list_ref.shape[1], step, 0, unroll=4)
    wait_sends(columns, me, send_ref, recv_ref, send_sems, recv_sems)


def one_tile(params, grads, length, centre_x, centre_y, before_ones, after_ones, moments):
    depth = params.shape[1]
    side = 16
    u = params[0:1] - centre_x
    v = params[1:2] - centre_y
    a = params[2:3]
    b = params[3:4]
    c = params[4:5]
    logit = params[5:6]
    local = lax.broadcasted_iota(jnp.int32, (side, depth), 0).astype(F32) - 7.5
    dx = local - u
    dy = local - v
    live = lax.broadcasted_iota(jnp.int32, (1, depth), 1) < length
    log_opacity = -(jnp.maximum(-logit, 0.0) + jnp.log(1.0 + jnp.exp(-jnp.abs(logit))))
    log_opacity = jnp.where(live, log_opacity * LOG2E, -1e30)
    part_x = (-0.5 * LOG2E) * (a * dx * dx)
    part_y = (-0.5 * LOG2E) * (c * dy * dy) + log_opacity
    cross = LOG2E * (b * dx)
    exponent = (part_x[None] + part_y[:, None]) - cross[None] * dy[:, None]
    exponent = exponent.reshape(side * side, depth)
    alpha = jnp.exp2(exponent)
    log_clear = jnp.log(1.0 - alpha) * LOG2E
    clear_high, clear_low = split2(log_clear)
    before = jnp.dot(clear_high, before_ones, preferred_element_type=F32) + jnp.dot(
        clear_low, before_ones, preferred_element_type=F32
    )
    weight = jnp.exp2(before) * alpha
    ratio = jnp.exp2(exponent - log_clear)
    grads_high, grads_low = split2(grads)
    colour_high, colour_low = split2(params[6:])
    pulled = lax.dot_general(
        jnp.concatenate([grads_high, grads_low, grads_high], axis=0),
        jnp.concatenate([colour_high, colour_high, colour_low], axis=0),
        (((0,), (0,)), ((), ())),
        preferred_element_type=F32,
    )
    flow = weight * pulled
    flow_high, flow_low = split2(flow)
    after = jnp.dot(flow_high, after_ones, preferred_element_type=F32) + jnp.dot(
        flow_low, after_ones, preferred_element_type=F32
    )
    change = flow - after * ratio
    weight_high, weight_low = split2(weight)
    both = jnp.dot(
        jnp.concatenate([grads_high, grads_low], axis=0),
        weight_high,
        preferred_element_type=F32,
    )
    channels = grads.shape[0]
    colour_grads = (both[:channels] + both[channels:]) + jnp.dot(
        grads_high, weight_low, preferred_element_type=F32
    )
    sums = sum(jnp.dot(moments, piece, preferred_element_type=F32) for piece in split3(change))
    m00, m10, m01, m20, m02, m11 = (sums[i : i + 1] for i in range(6))
    sx = m10 - u * m00
    sy = m01 - v * m00
    sxx = m20 - 2.0 * u * m10 + u * u * m00
    syy = m02 - 2.0 * v * m01 + v * v * m00
    sxy = m11 - u * m01 - v * m10 + u * v * m00
    closed = 1.0 / (1.0 + jnp.exp(logit))
    return jnp.concatenate(
        [
            a * sx + b * sy,
            c * sy + b * sx,
            -0.5 * sxx,
            -sxy,
            -0.5 * syy,
            m00 * closed,
            colour_grads,
        ],
        axis=0,
    )


def tile_kernel(per_step, length_ref, params_ref, grads_ref, out_ref):
    depth = out_ref.shape[1] // per_step
    first = pl.program_id(0) * per_step
    row_base = lax.axis_index("narrow") * (pl.num_programs(0) * per_step)
    centre_x = (lax.axis_index("wide") * 16 + 8).astype(F32)
    low = lax.broadcasted_iota(jnp.int32, (depth, depth), 0)
    high = lax.broadcasted_iota(jnp.int32, (depth, depth), 1)
    before_ones = (low < high).astype(F32).astype(BF16)
    after_ones = (low > high).astype(F32).astype(BF16)
    pixel = lax.broadcasted_iota(jnp.int32, (8, 256), 1)
    which = lax.broadcasted_iota(jnp.int32, (8, 256), 0)
    x = (pixel & 15).astype(F32) - 7.5
    y = (pixel >> 4).astype(F32) - 7.5
    moments = jnp.where(which == 0, 1.0, 0.0)
    for i, term in enumerate((x, y, x * x, y * y, x * y)):
        moments = jnp.where(which == i + 1, term, moments)
    moments = moments.astype(BF16)
    for i in range(per_step):
        centre_y = ((row_base + first + i) * 16 + 8).astype(F32)
        out_ref[:, i * depth : (i + 1) * depth] = one_tile(
            params_ref[:, i * depth : (i + 1) * depth],
            grads_ref[:, 0, i, :],
            length_ref[first + i],
            centre_x,
            centre_y,
            before_ones,
            after_ones,
            moments,
        )


SLOT_GROUP = 16
SPLAT_GROUP = 32
ENTRY_BLOCK = 2048


def scatter_group(group, size, blocks, spread_ref):
    total = jnp.zeros((size * 32, STRIP), F32)
    column = lax.broadcasted_iota(jnp.int32, (STRIP, ENTRY_BLOCK), 0)
    for load_index, load_values in blocks:
        index = load_index()
        strip = index >> 8
        hot = jnp.where(column == (index & (STRIP - 1)), 1.0, 0.0).astype(BF16)
        high, low = split2(load_values())
        both = jnp.concatenate([high, low], axis=0)
        for c in range(size):
            mask = jnp.where(strip == group * size + c, 1.0, 0.0).astype(BF16)
            spread_ref[c * 32 : (c + 1) * 32, :] = both * mask
        total += lax.dot_general(
            spread_ref[: size * 32, :], hot, (((1,), (1,)), ((), ())), preferred_element_type=F32
        )
    return [
        total[c * 32 : c * 32 + 16] + total[c * 32 + 16 : c * 32 + 32] for c in range(size)
    ]


def return_kernel(
    list_ref, value_ref, sent_ref, out_ref, spread_ref, send_ref, recv_ref, send_sems, recv_sems
):
    columns, _, cap = recv_ref.shape
    me = lax.axis_index("wide")
    barrier = greet(columns, me)
    half = columns // 2
    my_half = me // half
    depth = list_ref.shape[2]
    entry_blocks = [
        (
            lambda start=start: jnp.concatenate(
                [
                    list_ref[0, row : row + 1, :]
                    for row in range(start // depth, (start + ENTRY_BLOCK) // depth)
                ],
                axis=1,
            ),
            lambda start=start: value_ref[:, start : start + ENTRY_BLOCK],
        )
        for start in range(0, value_ref.shape[1], ENTRY_BLOCK)
    ]
    for phase in range(2):
        group = my_half if phase else 1 - my_half
        strips = scatter_group(group, SLOT_GROUP, entry_blocks, spread_ref)
        for c, rows in enumerate(strips):
            for part in range(STRIP // LANES):
                start = c * STRIP + part * LANES
                place = start % cap
                send_ref[group * half + start // cap, :, place : place + LANES] = rows[
                    :, part * LANES : (part + 1) * LANES
                ]
        if phase == 0:
            pl.semaphore_wait(barrier, columns - 1)

        def send(step, carry):
            peer = group * half + lax.rem(me + step, half)
            copy_between(send_ref, recv_ref, send_sems, recv_sems, peer, me).start()
            return carry

        lax.fori_loop(phase, half, send, 0)
    recv_ref[me] = send_ref[me]

    per_block = ENTRY_BLOCK // cap
    for phase in range(2):
        from_half = 1 - my_half if phase else my_half

        def arrived(step, carry):
            source = from_half * half + lax.rem(me + step, half)
            copy_between(send_ref, recv_ref, send_sems, recv_sems, source, source).wait_recv()
            return carry

        lax.fori_loop(1 - phase, half, arrived, 0)
        blocks = []
        for block in range(half // per_block):
            first = from_half * half + block * per_block
            blocks.append(
                (
                    lambda first=first: sent_ref[
                        0, :, pl.ds(pl.multiple_of(first * cap, LANES), ENTRY_BLOCK)
                    ],
                    lambda first=first: jnp.concatenate(
                        [recv_ref[first + i] for i in range(per_block)], axis=1
                    ),
                )
            )

        def splat_group(group, carry):
            found = scatter_group(group, SPLAT_GROUP, blocks, spread_ref)
            for c, rows in enumerate(found):
                where = pl.ds(pl.multiple_of((group * SPLAT_GROUP + c) * STRIP, STRIP), STRIP)
                out_ref[:, where] = rows if phase == 0 else out_ref[:, where] + rows
            return carry

        lax.fori_loop(0, out_ref.shape[1] // (SPLAT_GROUP * STRIP), splat_group, 0)
    wait_sends(columns, me, send_ref, recv_ref, send_sems, recv_sems)


def body(splats, send_slots, tile_lists, tile_lengths, pixel_grads):
    features, local_count = splats.shape
    slot_count = send_slots.shape[2]
    tile_count, depth = tile_lists.shape[1:]
    entry_count = tile_count * depth
    columns = lax.axis_size("wide")
    cap = slot_count // columns
    width = min(cap, STRIP)
    exchange = [
        pltpu.VMEM((columns, features, cap), F32),
        pltpu.VMEM((columns, features, cap), F32),
        pltpu.SemaphoreType.DMA((columns,)),
        pltpu.SemaphoreType.DMA((columns,)),
    ]
    all_params = pl.pallas_call(
        receive_kernel,
        out_shape=jax.ShapeDtypeStruct((features, entry_count), F32),
        in_specs=[whole(), whole(), whole()],
        out_specs=whole(),
        scratch_shapes=[
            pltpu.VMEM((local_count // STRIP // 2 * PAIR_ROWS, STRIP), BF16),
            pltpu.VMEM((slot_count // width // 2 * PAIR_ROWS, width), BF16),
        ]
        + exchange,
        compiler_params=pltpu.CompilerParams(
            vmem_limit_bytes=VMEM_BYTES, collective_id=0, has_side_effects=True
        ),
        name="receive_entries",
    )(
        send_slots,
        splats,
        tile_lists,
    )
    per_step = math.gcd(tile_count, 8)
    channels, pixels = pixel_grads.shape[0], pixel_grads.shape[3]
    entry_grads = pl.pallas_call(
        functools.partial(tile_kernel, per_step),
        out_shape=jax.ShapeDtypeStruct((features, entry_count), F32),
        grid=(tile_count // per_step,),
        in_specs=[
            pl.BlockSpec(memory_space=pltpu.SMEM),
            pl.BlockSpec((features, per_step * depth), lambda i: (0, i)),
            pl.BlockSpec((channels, 1, per_step, pixels), lambda i: (0, 0, i, 0)),
        ],
        out_specs=pl.BlockSpec((features, per_step * depth), lambda i: (0, i)),
        compiler_params=params_of(),
        name="tile_grads",
    )(tile_lengths.reshape(tile_count), all_params, pixel_grads)
    partial_grads = pl.pallas_call(
        return_kernel,
        out_shape=jax.ShapeDtypeStruct((features, local_count), F32),
        in_specs=[whole(), whole(), whole()],
        out_specs=whole(),
        scratch_shapes=[pltpu.VMEM((SPLAT_GROUP * 32, ENTRY_BLOCK), BF16)] + exchange,
        compiler_params=pltpu.CompilerParams(
            vmem_limit_bytes=VMEM_BYTES, collective_id=1, has_side_effects=True
        ),
        name="return_grads",
    )(
        tile_lists,
        entry_grads,
        send_slots,
    )
    other = lax.ppermute(partial_grads, "narrow", [(0, 1), (1, 0)])
    return partial_grads + other


def solution(mesh):
    placed = (
        P(None, ("groups", "wide")),
        P(("groups", "wide"), "narrow", None),
        P(("groups", "wide"), "narrow", None),
        P(("groups", "wide"), "narrow"),
        P(None, ("groups", "wide"), "narrow", None),
    )
    return jax.shard_map(
        body, mesh=mesh, in_specs=placed, out_specs=P(None, ("groups", "wide")), check_vma=False
    )
```

```python
import functools
import math

import jax
import jax.numpy as jnp
from jax import lax
from jax.experimental import pallas as pl
from jax.experimental.pallas import tpu as pltpu
from jax.sharding import PartitionSpec as P

LANES = 128
F32 = jnp.float32
BF16 = jnp.bfloat16
LOG2E = math.log2(math.e)
VMEM_BYTES = 48 * 1024 * 1024


def params_of():
    return pltpu.CompilerParams(vmem_limit_bytes=VMEM_BYTES)


def whole(*_):
    return pl.BlockSpec(memory_space=pltpu.VMEM)


def split2(values):
    high = values.astype(BF16)
    low = (values - high.astype(F32)).astype(BF16)
    return high, low


def split3(values):
    high = values.astype(BF16)
    rest = values - high.astype(F32)
    middle = rest.astype(BF16)
    low = (rest - middle.astype(F32)).astype(BF16)
    return high, middle, low


STRIP = 256
PAIR_ROWS = 80
PAIRS_PER_DOT = 2
MESH = pl.DeviceIdType.MESH


def spread_pair(first_strip, second_strip):
    first = split3(first_strip)
    second = split3(second_strip)
    low = jnp.concatenate([first[2].astype(F32)[:8], second[2].astype(F32)[:8]], axis=0)
    return jnp.concatenate([first[0], first[1], second[0], second[1], low.astype(BF16)], axis=0)


def gather_strip(index, spread_ref, first_pair, pair_count, strip_of):
    width = spread_ref.shape[1]
    count = index.shape[1]
    strip = jnp.broadcast_to(index // width, (8, count))
    column = lax.broadcasted_iota(jnp.int32, (width, count), 0)
    hot = jnp.where(column == (index & (width - 1)), 1.0, 0.0).astype(BF16)
    parts = [jnp.zeros((8, count), F32) for _ in range(5)]
    per_dot = min(PAIRS_PER_DOT, pair_count)
    rows = per_dot * PAIR_ROWS
    for block in range(pair_count // per_dot):
        start_row = first_pair * PAIR_ROWS + block * rows
        found = jnp.dot(
            spread_ref[start_row : start_row + rows, :], hot, preferred_element_type=F32
        )
        for p in range(per_dot):
            for q in range(2):
                here = strip == strip_of((first_pair + block * per_dot + p) * 2 + q)
                base = p * PAIR_ROWS
                starts = [base + q * 32 + 8 * i for i in range(4)] + [base + 64 + 8 * q]
                parts = [
                    jnp.where(here, found[start : start + 8], part)
                    for start, part in zip(starts, parts)
                ]
    return jnp.concatenate([parts[0] + (parts[2] + parts[4]), parts[1] + parts[3]], axis=0)


def copy_between(send_ref, recv_ref, send_sems, recv_sems, peer, mine):
    return pltpu.make_async_remote_copy(
        src_ref=send_ref.at[peer],
        dst_ref=recv_ref.at[mine],
        send_sem=send_sems.at[peer],
        recv_sem=recv_sems.at[mine],
        device_id={"wide": peer},
        device_id_type=MESH,
    )


def greet(columns, me):
    barrier = pltpu.get_barrier_semaphore()

    def hello(step, carry):
        peer = lax.rem(me + 1 + step, columns)
        pl.semaphore_signal(barrier, inc=1, device_id={"wide": peer}, device_id_type=MESH)
        return carry

    lax.fori_loop(0, columns - 1, hello, 0)
    return barrier


def wait_sends(columns, me, send_ref, recv_ref, send_sems, recv_sems):
    def done(step, carry):
        peer = lax.rem(me + 1 + step, columns)
        copy_between(send_ref, recv_ref, send_sems, recv_sems, peer, me).wait_send()
        return carry

    lax.fori_loop(0, columns - 1, done, 0)


def offset_of(step, columns):
    away = (step + 1) // 2
    return columns // 2 + away * (1 - 2 * (step % 2))


def receive_kernel(
    sent_ref, source_ref, list_ref, out_ref,
    spread_ref, spread_recv_ref, send_ref, recv_ref, send_sems, recv_sems,
):
    columns, _, cap = recv_ref.shape
    me = lax.axis_index("wide")
    barrier = greet(columns, me)
    source_strips = source_ref.shape[1] // STRIP
    for p in range(source_strips // 2):
        start = p * 2 * STRIP
        spread_ref[p * PAIR_ROWS : (p + 1) * PAIR_ROWS, :] = spread_pair(
            source_ref[:, start : start + STRIP], source_ref[:, start + STRIP : start + 2 * STRIP]
        )
    pl.semaphore_wait(barrier, columns - 1)
    width = min(cap, STRIP)
    per = cap // width

    def pick(peer, place):
        start = pl.multiple_of((peer * per + place) * width, width)
        index = sent_ref[0, :, pl.ds(start, width)]
        return gather_strip(index, spread_ref, 0, source_strips // 2, lambda strip: strip)

    def send(step, carry):
        peer = lax.rem(me + offset_of(step, columns), columns)
        for i in range(per):
            send_ref[peer, :, i * width : (i + 1) * width] = pick(peer, i)
        copy_between(send_ref, recv_ref, send_sems, recv_sems, peer, me).start()
        return carry

    lax.fori_loop(0, columns - 1, send, 0)
    for i in range(per):
        recv_ref[me, :, i * width : (i + 1) * width] = pick(me, i)

    half = columns // 2
    strips_half = half * per
    pairs_half = strips_half // 2
    sources = [lax.rem(me + columns - offset_of(k, columns), columns) for k in range(columns)]
    for phase in range(2):
        for k in range(phase * half, (phase + 1) * half):
            if k < columns - 1:
                copy_between(send_ref, recv_ref, send_sems, recv_sems, sources[k], sources[k]).wait_recv()
        strips = [
            (sources[phase * half + i // per], (i % per) * width) for i in range(strips_half)
        ]
        for p in range(pairs_half):
            blocks = [
                recv_ref[source, :, place : place + width]
                for source, place in strips[2 * p : 2 * p + 2]
            ]
            row = (phase * pairs_half + p) * PAIR_ROWS
            spread_recv_ref[row : row + PAIR_ROWS, :] = spread_pair(*blocks)

        def step(j, carry):
            found = gather_strip(
                list_ref[0, pl.ds(j, 1), :],
                spread_recv_ref,
                phase * pairs_half,
                pairs_half,
                lambda strip: sources[strip // per] * per + strip % per,
            )
            where = pl.ds(pl.multiple_of(j * STRIP, STRIP), STRIP)
            out_ref[:, where] = found if phase == 0 else out_ref[:, where] + found
            return carry

        lax.fori_loop(0, list_ref.shape[1], step, 0, unroll=4)
    wait_sends(columns, me, send_ref, recv_ref, send_sems, recv_sems)


def one_tile(params, grads, length, centre_x, centre_y, before_ones, after_ones, moments):
    depth = params.shape[1]
    side = 16
    u = params[0:1] - centre_x
    v = params[1:2] - centre_y
    a = params[2:3]
    b = params[3:4]
    c = params[4:5]
    logit = params[5:6]
    local = lax.broadcasted_iota(jnp.int32, (side, depth), 0).astype(F32) - 7.5
    dx = local - u
    dy = local - v
    live = lax.broadcasted_iota(jnp.int32, (1, depth), 1) < length
    log_opacity = -(jnp.maximum(-logit, 0.0) + jnp.log(1.0 + jnp.exp(-jnp.abs(logit))))
    log_opacity = jnp.where(live, log_opacity * LOG2E, -1e30)
    part_x = (-0.5 * LOG2E) * (a * dx * dx)
    part_y = (-0.5 * LOG2E) * (c * dy * dy) + log_opacity
    cross = LOG2E * (b * dx)
    exponent = (part_x[None] + part_y[:, None]) - cross[None] * dy[:, None]
    exponent = exponent.reshape(side * side, depth)
    alpha = jnp.exp2(exponent)
    log_clear = jnp.log(1.0 - alpha) * LOG2E
    clear_high, clear_low = split2(log_clear)
    before = jnp.dot(clear_high, before_ones, preferred_element_type=F32) + jnp.dot(
        clear_low, before_ones, preferred_element_type=F32
    )
    weight = jnp.exp2(before) * alpha
    ratio = jnp.exp2(exponent - log_clear)
    grads_high, grads_low = split2(grads)
    colour_high, colour_low = split2(params[6:])
    pulled = lax.dot_general(
        jnp.concatenate([grads_high, grads_low, grads_high], axis=0),
        jnp.concatenate([colour_high, colour_high, colour_low], axis=0),
        (((0,), (0,)), ((), ())),
        preferred_element_type=F32,
    )
    flow = weight * pulled
    flow_high, flow_low = split2(flow)
    after = jnp.dot(flow_high, after_ones, preferred_element_type=F32) + jnp.dot(
        flow_low, after_ones, preferred_element_type=F32
    )
    change = flow - after * ratio
    weight_high, weight_low = split2(weight)
    both = jnp.dot(
        jnp.concatenate([grads_high, grads_low], axis=0),
        weight_high,
        preferred_element_type=F32,
    )
    channels = grads.shape[0]
    colour_grads = (both[:channels] + both[channels:]) + jnp.dot(
        grads_high, weight_low, preferred_element_type=F32
    )
    sums = sum(jnp.dot(moments, piece, preferred_element_type=F32) for piece in split3(change))
    m00, m10, m01, m20, m02, m11 = (sums[i : i + 1] for i in range(6))
    sx = m10 - u * m00
    sy = m01 - v * m00
    sxx = m20 - 2.0 * u * m10 + u * u * m00
    syy = m02 - 2.0 * v * m01 + v * v * m00
    sxy = m11 - u * m01 - v * m10 + u * v * m00
    closed = 1.0 / (1.0 + jnp.exp(logit))
    return jnp.concatenate(
        [
            a * sx + b * sy,
            c * sy + b * sx,
            -0.5 * sxx,
            -sxy,
            -0.5 * syy,
            m00 * closed,
            colour_grads,
        ],
        axis=0,
    )


def tile_kernel(per_step, length_ref, params_ref, grads_ref, out_ref):
    depth = out_ref.shape[1] // per_step
    first = pl.program_id(0) * per_step
    row_base = lax.axis_index("narrow") * (pl.num_programs(0) * per_step)
    centre_x = (lax.axis_index("wide") * 16 + 8).astype(F32)
    low = lax.broadcasted_iota(jnp.int32, (depth, depth), 0)
    high = lax.broadcasted_iota(jnp.int32, (depth, depth), 1)
    before_ones = (low < high).astype(F32).astype(BF16)
    after_ones = (low > high).astype(F32).astype(BF16)
    pixel = lax.broadcasted_iota(jnp.int32, (8, 256), 1)
    which = lax.broadcasted_iota(jnp.int32, (8, 256), 0)
    x = (pixel & 15).astype(F32) - 7.5
    y = (pixel >> 4).astype(F32) - 7.5
    moments = jnp.where(which == 0, 1.0, 0.0)
    for i, term in enumerate((x, y, x * x, y * y, x * y)):
        moments = jnp.where(which == i + 1, term, moments)
    moments = moments.astype(BF16)
    for i in range(per_step):
        centre_y = ((row_base + first + i) * 16 + 8).astype(F32)
        out_ref[:, i * depth : (i + 1) * depth] = one_tile(
            params_ref[:, i * depth : (i + 1) * depth],
            grads_ref[:, 0, i, :],
            length_ref[first + i],
            centre_x,
            centre_y,
            before_ones,
            after_ones,
            moments,
        )


SLOT_GROUP = 8
SPLAT_GROUP = 32
ENTRY_BLOCK = 2048


def scatter_group(group, size, blocks, spread_ref):
    total = jnp.zeros((size * 32, STRIP), F32)
    column = lax.broadcasted_iota(jnp.int32, (STRIP, ENTRY_BLOCK), 0)
    for load_index, load_values in blocks:
        index = load_index()
        strip = index >> 8
        hot = jnp.where(column == (index & (STRIP - 1)), 1.0, 0.0).astype(BF16)
        high, low = split2(load_values())
        both = jnp.concatenate([high, low], axis=0)
        for c in range(size):
            mask = jnp.where(strip == group * size + c, 1.0, 0.0).astype(BF16)
            spread_ref[c * 32 : (c + 1) * 32, :] = both * mask
        total += lax.dot_general(
            spread_ref[: size * 32, :], hot, (((1,), (1,)), ((), ())), preferred_element_type=F32
        )
    return [
        total[c * 32 : c * 32 + 16] + total[c * 32 + 16 : c * 32 + 32] for c in range(size)
    ]


def return_kernel(
    list_ref, value_ref, sent_ref, out_ref, spread_ref, send_ref, recv_ref, send_sems, recv_sems
):
    columns, _, cap = recv_ref.shape
    me = lax.axis_index("wide")
    barrier = greet(columns, me)
    half = columns // 2
    my_half = me // half
    depth = list_ref.shape[2]
    entry_blocks = [
        (
            lambda start=start: jnp.concatenate(
                [
                    list_ref[0, row : row + 1, :]
                    for row in range(start // depth, (start + ENTRY_BLOCK) // depth)
                ],
                axis=1,
            ),
            lambda start=start: value_ref[:, start : start + ENTRY_BLOCK],
        )
        for start in range(0, value_ref.shape[1], ENTRY_BLOCK)
    ]
    quarter = columns // 4
    mine = me // quarter
    beside = mine + 1 - 2 * lax.rem(mine, 2)
    order = [lax.rem(mine + 2, 4), lax.rem(beside + 2, 4), beside, mine]
    for part_at, group in enumerate(order):
        strips = scatter_group(group, SLOT_GROUP, entry_blocks, spread_ref)
        for c, rows in enumerate(strips):
            for part in range(STRIP // LANES):
                start = c * STRIP + part * LANES
                place = start % cap
                send_ref[group * quarter + start // cap, :, place : place + LANES] = rows[
                    :, part * LANES : (part + 1) * LANES
                ]
        if part_at == 0:
            pl.semaphore_wait(barrier, columns - 1)

        def send(step, carry):
            peer = group * quarter + lax.rem(me + step, quarter)
            copy_between(send_ref, recv_ref, send_sems, recv_sems, peer, me).start()
            return carry

        lax.fori_loop(part_at // 3, quarter, send, 0)
    recv_ref[me] = send_ref[me]

    per_block = ENTRY_BLOCK // cap
    for phase in range(2):
        from_half = 1 - my_half if phase else my_half

        def arrived(step, carry):
            source = from_half * half + lax.rem(me + step, half)
            copy_between(send_ref, recv_ref, send_sems, recv_sems, source, source).wait_recv()
            return carry

        lax.fori_loop(1 - phase, half, arrived, 0)
        blocks = []
        for block in range(half // per_block):
            first = from_half * half + block * per_block
            blocks.append(
                (
                    lambda first=first: sent_ref[
                        0, :, pl.ds(pl.multiple_of(first * cap, LANES), ENTRY_BLOCK)
                    ],
                    lambda first=first: jnp.concatenate(
                        [recv_ref[first + i] for i in range(per_block)], axis=1
                    ),
                )
            )

        def splat_group(group, carry):
            found = scatter_group(group, SPLAT_GROUP, blocks, spread_ref)
            for c, rows in enumerate(found):
                where = pl.ds(pl.multiple_of((group * SPLAT_GROUP + c) * STRIP, STRIP), STRIP)
                out_ref[:, where] = rows if phase == 0 else out_ref[:, where] + rows
            return carry

        lax.fori_loop(0, out_ref.shape[1] // (SPLAT_GROUP * STRIP), splat_group, 0)
    wait_sends(columns, me, send_ref, recv_ref, send_sems, recv_sems)


def body(splats, send_slots, tile_lists, tile_lengths, pixel_grads):
    features, local_count = splats.shape
    slot_count = send_slots.shape[2]
    tile_count, depth = tile_lists.shape[1:]
    entry_count = tile_count * depth
    columns = lax.axis_size("wide")
    cap = slot_count // columns
    width = min(cap, STRIP)
    exchange = [
        pltpu.VMEM((columns, features, cap), F32),
        pltpu.VMEM((columns, features, cap), F32),
        pltpu.SemaphoreType.DMA((columns,)),
        pltpu.SemaphoreType.DMA((columns,)),
    ]
    all_params = pl.pallas_call(
        receive_kernel,
        out_shape=jax.ShapeDtypeStruct((features, entry_count), F32),
        in_specs=[whole(), whole(), whole()],
        out_specs=whole(),
        scratch_shapes=[
            pltpu.VMEM((local_count // STRIP // 2 * PAIR_ROWS, STRIP), BF16),
            pltpu.VMEM((slot_count // width // 2 * PAIR_ROWS, width), BF16),
        ]
        + exchange,
        compiler_params=pltpu.CompilerParams(
            vmem_limit_bytes=VMEM_BYTES, collective_id=0, has_side_effects=True
        ),
        name="receive_entries",
    )(
        send_slots,
        splats,
        tile_lists,
    )
    per_step = math.gcd(tile_count, 8)
    channels, pixels = pixel_grads.shape[0], pixel_grads.shape[3]
    entry_grads = pl.pallas_call(
        functools.partial(tile_kernel, per_step),
        out_shape=jax.ShapeDtypeStruct((features, entry_count), F32),
        grid=(tile_count // per_step,),
        in_specs=[
            pl.BlockSpec(memory_space=pltpu.SMEM),
            pl.BlockSpec((features, per_step * depth), lambda i: (0, i)),
            pl.BlockSpec((channels, 1, per_step, pixels), lambda i: (0, 0, i, 0)),
        ],
        out_specs=pl.BlockSpec((features, per_step * depth), lambda i: (0, i)),
        compiler_params=params_of(),
        name="tile_grads",
    )(tile_lengths.reshape(tile_count), all_params, pixel_grads)
    partial_grads = pl.pallas_call(
        return_kernel,
        out_shape=jax.ShapeDtypeStruct((features, local_count), F32),
        in_specs=[whole(), whole(), whole()],
        out_specs=whole(),
        scratch_shapes=[pltpu.VMEM((SPLAT_GROUP * 32, ENTRY_BLOCK), BF16)] + exchange,
        compiler_params=pltpu.CompilerParams(
            vmem_limit_bytes=VMEM_BYTES, collective_id=1, has_side_effects=True
        ),
        name="return_grads",
    )(
        tile_lists,
        entry_grads,
        send_slots,
    )
    other = lax.ppermute(partial_grads, "narrow", [(0, 1), (1, 0)])
    return partial_grads + other


def solution(mesh):
    placed = (
        P(None, ("groups", "wide")),
        P(("groups", "wide"), "narrow", None),
        P(("groups", "wide"), "narrow", None),
        P(("groups", "wide"), "narrow"),
        P(None, ("groups", "wide"), "narrow", None),
    )
    return jax.shard_map(
        body, mesh=mesh, in_specs=placed, out_specs=P(None, ("groups", "wide")), check_vma=False
    )
```
